32 devices in a mesh: job: 2 (over y), dp: 4 (over x, core), panel: 4 (over z).
Axes of the slice: x: 2, y: 2, z: 4, core: 2. Of those that a mesh axis runs over, the one named last changes fastest.
Arguments:
- acts: bfloat16 [4096, 8192], P(('job', 'dp')), parts along dimension 0, may hold values from -6 to 6
- cotangent: bfloat16 [4096, 28672], P(('job', 'dp'), 'panel'), parts along dimension 0, may hold values from -0.3125 to 0.3125
- down_factor_rows: bfloat16 [32, 8192], P('job'), parts along dimension 0, may hold values from -0.0625 to 0.0625
- up_factor_matrix: bfloat16 [32, 28672], P('job', 'panel'), parts along dimension 0, may hold values from -0.03125 to 0.03125
- slot_block_rows: int32 [8, 8], P(('job', 'panel')), parts along dimension 0, may hold values from 0 to 63, as said below
- panel_block_columns: int32 [8, 8], P(('job', 'panel')), parts along dimension 0, may hold values from 0 to 55, as said below
- panel_live_count: int32 [8], P(('job', 'panel')), parts along dimension 0, may hold values from 2 to 8, as said below
Outputs:
- block_grads: float32 [8, 8, 128, 128], P(('job', 'panel'), 'dp'), parts along dimension 0
- grad_down: float32 [32, 8192], P('job', 'panel'), parts along dimension 0
- grad_up: float32 [32, 28672], P('job', 'panel'), parts along dimension 0
The draws below stay inside these ranges and needn't reach their ends.
There are 2 independent parts, one for each index of `job`. The reference program is written for one: setup_inputs(seed, part) draws one part's arguments, and reference() takes and returns one part's arrays. A program takes and returns all parts, laid end to end along the dimension named above; each array names one. Nothing has to cross between parts.
Inputs may be any that keep to these rules, and one draw needn't show every extreme that they name: `slot_block_rows`: row block indices of the slots. Column block indices within the panel; within one panel the 8 pairs (slot_block_rows, panel_block_columns) are all different. Only the first panel_live_count[p] slots of panel p are live; some panel has all 8 slots live.
All inputs are finite; a program needn't handle non-finite values.
Results may differ from the reference program's by a relative error of at most 0.0029.
Values may be sent and summed in bfloat16 or wider, within the bound.
No kernel may reach another device: no remote copies, remote signals or barrier semaphores. Data moves between devices by JAX's collectives and lax.ppermute only.
A program may use at most 128 MiB of HBM per device.

```python
import jax
import jax.numpy as jnp
from jax import lax

MODEL_WIDTH = 8192
HIDDEN_UNITS = 28672
ADAPTER_RANK = 16
BLK = 128
TOKENS = 2048
SLOTS = 8
N_PANEL = 4


def block_table(key):
    row_blocks = MODEL_WIDTH // BLK
    col_blocks = HIDDEN_UNITS // (BLK * N_PANEL)
    panel_keys = jax.random.split(key, N_PANEL)

    def one_panel(panel_key):
        return jax.random.permutation(panel_key, row_blocks * col_blocks)[:SLOTS]
    return (jax.vmap(one_panel)(panel_keys).astype(jnp.int32), col_blocks)


def draw_slot_block_rows(key, part):
    places, col_blocks = block_table(key)
    return (places // col_blocks).astype(jnp.int32)


def draw_panel_block_columns(key, part):
    places, col_blocks = block_table(key)
    return (places % col_blocks).astype(jnp.int32)


def draw_panel_live_count(key, part):
    key = jax.random.fold_in(key, 3)
    counts = jax.random.randint(key, (N_PANEL,), max(1, SLOTS // 3), SLOTS + 1)
    fuller = jax.random.randint(jax.random.fold_in(key, 7), (), 0, N_PANEL)
    counts = jnp.where(jnp.arange(N_PANEL) == fuller, SLOTS, counts)
    return counts.astype(jnp.int32)


def block_levels(rng, shape, pieces, smallest, top_value):
    def one(position, parts):
        heights = jax.random.uniform(jax.random.fold_in(jax.random.fold_in(rng, 6), position), (parts,), jnp.float32, smallest / len(pieces), top_value / len(pieces))
        return jnp.repeat(jnp.exp(heights), shape[position] // parts).reshape((-1,) + (1,) * (len(shape) - position - 1))

    level = one(*pieces[0])
    for cut in pieces[1:]:
        level = level * one(*cut)
    return level


def gaussian(key, dims, width, most, cuts=(), kind=jnp.bfloat16):
    array = jax.random.normal(key, dims, jnp.float32) * width
    if len(cuts) > 0:
        array = block_levels(key, dims, cuts, -0.22, 0.18) * array
    return jnp.clip(array, min=-most, max=most).astype(kind)


def setup_inputs(seed: int = 0, part: int = 0) -> dict:
    seeds = jax.random.split(jax.random.key(seed), 8)
    part_splits = jax.random.split(jax.random.fold_in(seeds[7], part), 8)
    acts = gaussian(part_splits[0], (TOKENS, MODEL_WIDTH), 1.0, 6.0, ((0, 4),))
    cotangent = gaussian(part_splits[1], (TOKENS, HIDDEN_UNITS), (TOKENS ** -0.5), 0.3125, ((0, 4), (1, 4)))
    down_factor_rows = gaussian(part_splits[2], (ADAPTER_RANK, MODEL_WIDTH), MODEL_WIDTH ** -0.5, 0.0625)
    up_factor_matrix = gaussian(part_splits[3], (ADAPTER_RANK, HIDDEN_UNITS), HIDDEN_UNITS ** -0.5, 0.03125, ((1, 4),))
    slot_block_rows = draw_slot_block_rows(jax.random.fold_in(jax.random.fold_in(seeds[7], part), 71), part)
    panel_block_columns = draw_panel_block_columns(jax.random.fold_in(jax.random.fold_in(seeds[7], part), 71), part)
    panel_live_count = draw_panel_live_count(jax.random.fold_in(jax.random.fold_in(seeds[7], part), 71), part)
    return dict(acts=acts, cotangent=cotangent, down_factor_rows=down_factor_rows, up_factor_matrix=up_factor_matrix, slot_block_rows=slot_block_rows, panel_block_columns=panel_block_columns, panel_live_count=panel_live_count)


def reference(acts, cotangent, down_factor_rows, up_factor_matrix, slot_block_rows, panel_block_columns, panel_live_count):
    row_blocks = MODEL_WIDTH // BLK
    col_blocks = HIDDEN_UNITS // (BLK * N_PANEL)
    act_blocks = acts.reshape(TOKENS, row_blocks, BLK)

    def panel_grads(inputs):
        panel_index, slot_rows, slot_cols, live_count = inputs
        start = (panel_index * (col_blocks * BLK)).astype(jnp.int32)
        cot_panel = lax.dynamic_slice_in_dim(cotangent, start, col_blocks * BLK, 1)
        cot_blocks = cot_panel.reshape(TOKENS, col_blocks, BLK)
        act_picked = jnp.take(act_blocks, slot_rows, axis=1).astype(jnp.float32)
        cot_picked = jnp.take(cot_blocks, slot_cols, axis=1).astype(jnp.float32)
        products = jnp.einsum('tsa,tsb->sab', act_picked, cot_picked)
        live_slots = jnp.arange(SLOTS, dtype=jnp.int32) < live_count
        return jnp.where(live_slots[:, None, None], products, jnp.float32(0.0))

    block_grads = lax.map(panel_grads, (jnp.arange(N_PANEL, dtype=jnp.int32), slot_block_rows, panel_block_columns, panel_live_count))
    lowrank_input = jnp.dot(acts, down_factor_rows.T, preferred_element_type=jnp.float32).astype(jnp.bfloat16)
    backward_projection = jnp.dot(cotangent, up_factor_matrix.T, preferred_element_type=jnp.float32).astype(jnp.bfloat16)
    grad_down = jnp.dot(backward_projection.T, acts, preferred_element_type=jnp.float32)
    grad_up = jnp.dot(lowrank_input.T, cotangent, preferred_element_type=jnp.float32)
    return (block_grads, grad_down, grad_up)
```

```python
import functools

import jax
import jax.numpy as jnp
from jax import lax
from jax.experimental import pallas as pl
from jax.experimental.pallas import tpu as pltpu
from jax.sharding import PartitionSpec as P

BLK = 128
COT_CHUNK = 512
ACT_CHUNK = 1024
LAST_LAST = (((1,), (1,)), ((), ()))
LAST_FIRST = (((1,), (0,)), ((), ()))
FIRST_FIRST = (((0,), (0,)), ((), ()))
IN_HBM = pl.BlockSpec(memory_space=pltpu.HBM)
IN_VMEM = pl.BlockSpec(memory_space=pltpu.VMEM)
IN_SMEM = pl.BlockSpec(memory_space=pltpu.SMEM)


def dot(a, b, dims):
    return lax.dot_general(a, b, dims, preferred_element_type=jnp.float32)


def call(kernel, outs, specs, args, scratch=(), flops=0, moved=0):
    return pl.pallas_call(
        kernel,
        out_shape=outs,
        in_specs=specs,
        out_specs=jax.tree.map(lambda _: IN_VMEM, outs),
        scratch_shapes=scratch,
        cost_estimate=pl.CostEstimate(flops=flops, bytes_accessed=moved, transcendentals=0),
        compiler_params=pltpu.CompilerParams(vmem_limit_bytes=16 * 2**20),
    )(*args)


def back_kernel(cot, up, back, cot_here, up_here, sems):
    width = cot.shape[1]
    step = min(COT_CHUNK, width)
    count = width // step
    first = pltpu.make_async_copy(up, up_here, sems.at[count])
    first.start()
    copies = []
    for j in range(count):
        cols = pl.ds(j * step, step)
        copies.append(pltpu.make_async_copy(cot.at[:, cols], cot_here.at[:, cols], sems.at[j]))
        copies[-1].start()
    first.wait()
    total = None
    for j in range(count):
        cols = pl.ds(j * step, step)
        copies[j].wait()
        part = dot(up_here[:, cols], cot_here[:, cols], LAST_LAST)
        total = part if total is None else total + part
    back[...] = total


def low_kernel(rows, cols, acts, down, cot, grad_up, blocks):
    low = dot(down[...], acts[...], LAST_LAST).astype(jnp.bfloat16)
    grad_up[...] = dot(low, cot[...], LAST_FIRST)
    for s in range(blocks.shape[0]):
        r = pl.ds(pl.multiple_of(rows[0, s] * BLK, BLK), BLK)
        c = pl.ds(pl.multiple_of(cols[0, s] * BLK, BLK), BLK)
        blocks[s] = dot(acts[:, r], cot[:, c], FIRST_FIRST)


def down_kernel(back, acts, panel, out):
    width = out.shape[1]
    mine = pl.ds(pl.multiple_of(panel[0] * width, width), width)
    out[...] = dot(back[...].astype(jnp.bfloat16), acts[:, mine], LAST_FIRST)


def swap(x, axis, bit):
    return lax.ppermute(x, axis, [(i, i ^ bit) for i in range(lax.axis_size(axis))])


def body(acts, cot, down, up, rows, cols, live):
    tokens, width = acts.shape
    features = cot.shape[1]
    slots = rows.shape[1]
    dp, panels = lax.axis_size("dp"), lax.axis_size("panel")
    me = lax.axis_index("dp")
    own = slots // dp
    f32 = jnp.float32
    far = [1 << b for b in range(1, dp.bit_length() - 1)]
    wire = jnp.bfloat16 if len(far) == 1 else f32
    rank = down.shape[0]
    half = rank // 2
    core = me % 2

    hbm = functools.partial(pltpu.with_memory_space_constraint, memory_space=pltpu.HBM)
    vmem = functools.partial(pltpu.with_memory_space_constraint, memory_space=pltpu.VMEM)
    steps = max(1, features // COT_CHUNK)
    back, cot_here = call(
        back_kernel,
        (pltpu.VMEM((rank, tokens), f32), pltpu.VMEM((tokens, features), jnp.bfloat16)),
        [IN_HBM, IN_HBM],
        (hbm(cot), hbm(up)),
        [pltpu.VMEM((rank, features), jnp.bfloat16), pltpu.SemaphoreType.DMA((steps + 1,))],
        flops=2 * 256 * tokens * features,
        moved=2 * tokens * features,
    )
    acts_here = vmem(acts)
    grad_up, blocks = call(
        low_kernel,
        (pltpu.VMEM((rank, features), f32), pltpu.VMEM((slots, BLK, BLK), f32)),
        [IN_SMEM, IN_SMEM, IN_VMEM, IN_VMEM, IN_VMEM],
        (rows, cols, acts_here, down, cot_here),
        flops=2 * 256 * tokens * (features + width),
        moved=2 * tokens * width,
    )
    bit = 1
    while bit < panels:
        back = back + swap(back, "panel", bit)
        bit *= 2
    grad_down = call(
        down_kernel,
        pltpu.VMEM((rank, width // panels), f32),
        [IN_VMEM, IN_VMEM, IN_SMEM],
        (back, acts_here, lax.axis_index("panel").astype(jnp.int32)[None]),
        flops=2 * 256 * tokens * width // panels,
        moved=2 * tokens * width // panels,
    )

    def reduce_scatter_rows(x):
        mine = lax.dynamic_slice_in_dim(x, core * half, half, 0)
        other = lax.dynamic_slice_in_dim(x, (1 - core) * half, half, 0)
        return mine + swap(other, "dp", 1)

    def far_sum(x):
        for b in far:
            y = x.astype(wire)
            x = y.astype(f32) + swap(y, "dp", b).astype(f32)
        return x

    def gather_rows(x):
        other = swap(x, "dp", 1)
        both = jnp.where(core == 0, jnp.concatenate([x, other]), jnp.concatenate([other, x]))
        return both

    blocks = blocks.reshape(dp // 2, 2, own, BLK, BLK)
    pick = lambda x, i, axis: lax.dynamic_index_in_dim(x, i, axis, keepdims=False)
    blocks = pick(blocks, core, 1) + swap(pick(blocks, 1 - core, 1), "dp", 1)
    for b in reversed(far):
        count = blocks.shape[0] // 2
        split = blocks.reshape(2, count, own, BLK, BLK)
        side = (me // b) % 2
        sent = swap(pick(split, 1 - side, 0).astype(wire), "dp", b)
        blocks = pick(split, side, 0) + sent.astype(f32)
    blocks = blocks.reshape(own, BLK, BLK)
    alive = me * own + jnp.arange(own, dtype=jnp.int32) < live[0]
    blocks = jnp.where(alive[:, None, None], blocks, f32(0.0))[None]

    grad_up = gather_rows(far_sum(reduce_scatter_rows(grad_up)))
    grad_down = gather_rows(far_sum(reduce_scatter_rows(grad_down)))
    return blocks, grad_down, grad_up


def solution(mesh):
    in_specs = (
        P(("job", "dp"), None),
        P(("job", "dp"), "panel"),
        P("job", None),
        P("job", "panel"),
        P(("job", "panel"), None),
        P(("job", "panel"), None),
        P(("job", "panel")),
    )
    out_specs = (P(("job", "panel"), "dp", None, None), P("job", "panel"), P("job", "panel"))
    return jax.shard_map(body, mesh=mesh, in_specs=in_specs, out_specs=out_specs, check_vma=False)
```

```python
import functools
import itertools

import jax
import jax.numpy as jnp
from jax import lax
from jax.experimental import pallas as pl
from jax.experimental.pallas import tpu as pltpu
from jax.sharding import PartitionSpec as P

BLK = 128
COT_CHUNK = 1024
AHEAD = 5
RADIX = 4
CROSS = 1
ACT_CHUNK = 1024
LAST_LAST = (((1,), (1,)), ((), ()))
LAST_FIRST = (((1,), (0,)), ((), ()))
FIRST_FIRST = (((0,), (0,)), ((), ()))
IN_HBM = pl.BlockSpec(memory_space=pltpu.HBM)
IN_VMEM = pl.BlockSpec(memory_space=pltpu.VMEM)


def dot(a, b, dims):
    return lax.dot_general(a, b, dims, preferred_element_type=jnp.float32)


def call(kernel, outs, specs, args, scratch=(), vmem=16, flops=0, moved=0):
    return pl.pallas_call(
        kernel,
        out_shape=outs,
        in_specs=specs,
        out_specs=jax.tree.map(lambda _: IN_VMEM, outs),
        scratch_shapes=scratch,
        cost_estimate=pl.CostEstimate(flops=flops, bytes_accessed=moved, transcendentals=0),
        compiler_params=pltpu.CompilerParams(vmem_limit_bytes=vmem * 2**20),
    )(*args)


def local_kernel(rows_hbm, cols_hbm, acts, cot, down, up, up_mine, up_other, blocks_mine, blocks_other, back,
                 acts_mine, rows, cols, acts_here, cot_here, down_here, up_here, act_sems, cot_sems, sems):
    core = lax.rem(lax.axis_index("dp"), 2)
    width, features, mine = acts.shape[1], cot.shape[1], acts_mine.shape[1]
    act_step, cot_step = min(ACT_CHUNK, width), min(COT_CHUNK, features)

    def stream(source, target, step, sem):
        chunks = [pl.ds(j * step, step) for j in range(source.shape[1] // step)]
        return [pltpu.make_async_copy(source.at[:, at], target.at[:, at], sem.at[j]) for j, at in enumerate(chunks)]

    factors = [
        pltpu.make_async_copy(down, down_here, sems.at[0]),
        pltpu.make_async_copy(up, up_here, sems.at[1]),
        pltpu.make_async_copy(rows_hbm, rows, sems.at[3]),
        pltpu.make_async_copy(cols_hbm, cols, sems.at[4]),
    ]
    act_copies = stream(acts, acts_here, act_step, act_sems)
    cot_copies = stream(cot, cot_here, cot_step, cot_sems)
    order = factors + act_copies + cot_copies
    for copy in order[: AHEAD + len(factors)]:
        copy.start()
    waiting = iter(order[AHEAD + len(factors) :])

    def arrive(copy):
        copy.wait()
        for later in itertools.islice(waiting, 1):
            later.start()

    for copy in factors:
        copy.wait()
    low = None
    for j, copy in enumerate(act_copies):
        arrive(copy)
        at = pl.ds(j * act_step, act_step)
        part = dot(down_here[:, at], acts_here[:, at], LAST_LAST)
        low = part if low is None else low + part
    low = low.astype(jnp.bfloat16)
    slice_at = pl.ds(pl.multiple_of(lax.axis_index("panel") * mine, mine), mine)
    keep = pltpu.make_async_copy(acts_here.at[:, slice_at], acts_mine, sems.at[2])
    keep.start()
    total = None
    for j, copy in enumerate(cot_copies):
        arrive(copy)
        at = pl.ds(j * cot_step, cot_step)
        part = dot(up_here[:, at], cot_here[:, at], LAST_LAST)
        total = part if total is None else total + part
        part = dot(low, cot_here[:, at], LAST_FIRST)
        first, second = part[: part.shape[0] // 2], part[part.shape[0] // 2 :]
        up_mine[:, at] = jnp.where(core == 0, first, second)
        up_other[:, at] = jnp.where(core == 0, second, first)
    back[...] = total
    chips, own = blocks_mine.shape[:2]
    for out, owner in ((blocks_other, 1 - core), (blocks_mine, core)):
        for chip in range(chips):
            for k in range(own):
                s = (2 * chip + owner) * own + k
                r = pl.ds(pl.multiple_of(rows[0, s] * BLK, BLK), BLK)
                c = pl.ds(pl.multiple_of(cols[0, s] * BLK, BLK), BLK)
                out[chip, k] = dot(acts_here[:, r], cot_here[:, c], FIRST_FIRST)
    keep.wait()


def down_kernel(*refs):
    *shares, acts, out = refs
    back = shares[0][...]
    for share in shares[1:]:
        back = back + share[...]
    out[...] = dot(back.astype(jnp.bfloat16), acts[...], LAST_FIRST)


def swap(x, axis, bits):
    return lax.ppermute(x, axis, [(i, i ^ bits) for i in range(lax.axis_size(axis))])


def body(acts, cot, down, up, rows, cols, live):
    tokens, width = acts.shape
    features = cot.shape[1]
    slots = rows.shape[1]
    rank = down.shape[0]
    dp, panels = lax.axis_size("dp"), lax.axis_size("panel")
    me = lax.axis_index("dp")
    core, own, mine = me % 2, slots // dp, width // panels
    f32, bf16 = jnp.float32, jnp.bfloat16
    far = [1 << b for b in range(1, dp.bit_length() - 1)]
    wire = bf16 if len(far) == 1 else f32

    hbm = functools.partial(pltpu.with_memory_space_constraint, memory_space=pltpu.HBM)
    half = rank // 2
    up_sum, up_other, blocks, blocks_other, back, acts_mine = call(
        local_kernel,
        (
            pltpu.VMEM((half, features), f32),
            pltpu.VMEM((half, features), f32),
            pltpu.VMEM((dp // 2, own, BLK, BLK), f32),
            pltpu.VMEM((dp // 2, own, BLK, BLK), f32),
            pltpu.VMEM((rank, tokens), f32),
            pltpu.VMEM((tokens, mine), bf16),
        ),
        [IN_HBM] * 6,
        (hbm(rows), hbm(cols), hbm(acts), hbm(cot), hbm(down), hbm(up)),
        [
            pltpu.SMEM((1, slots), jnp.int32),
            pltpu.SMEM((1, slots), jnp.int32),
            pltpu.VMEM((tokens, width), bf16),
            pltpu.VMEM((tokens, features), bf16),
            pltpu.VMEM((rank, width), bf16),
            pltpu.VMEM((rank, features), bf16),
            pltpu.SemaphoreType.DMA((width // min(ACT_CHUNK, width),)),
            pltpu.SemaphoreType.DMA((features // min(COT_CHUNK, features),)),
            pltpu.SemaphoreType.DMA((5,)),
        ],
        vmem=24,
        flops=2 * 256 * tokens * (2 * features + width),
        moved=2 * tokens * (features + width),
    )

    pick = lambda x, i, axis: lax.dynamic_index_in_dim(x, i, axis, keepdims=False)
    gu = up_sum + swap(up_other, "dp", 1)
    for b in far:
        sent = gu.astype(wire)
        gu = sent.astype(f32) + swap(sent, "dp", b).astype(f32)
    other = swap(gu, "dp", 1)
    grad_up = jnp.where(core == 0, jnp.concatenate([gu, other]), jnp.concatenate([other, gu]))

    blocks = blocks + swap(blocks_other, "dp", 1)
    for b in reversed(far):
        split = blocks.reshape(2, blocks.shape[0] // 2, own, BLK, BLK)
        side = (me // b) % 2
        sent = swap(pick(split, 1 - side, 0).astype(wire), "dp", b)
        blocks = pick(split, side, 0) + sent.astype(f32)
    blocks = blocks.reshape(own, BLK, BLK)
    alive = me * own + jnp.arange(own, dtype=jnp.int32) < live[0]
    blocks = jnp.where(alive[:, None, None], blocks, f32(0.0))[None]

    bit, shares = 1, [back]
    while bit < panels:
        base = functools.reduce(jnp.add, shares)
        radix = min(RADIX, panels // bit)
        shares = [base] + [swap(base, "panel", k * bit) for k in range(1, radix)]
        bit *= radix
    gd = call(
        down_kernel,
        pltpu.VMEM((rank, mine), f32),
        [IN_VMEM] * (len(shares) + 1),
        (*shares, acts_mine),
        flops=2 * 256 * tokens * mine,
        moved=2 * tokens * mine,
    )
    gd = gd + swap(gd, "dp", 1)
    for b in far:
        sent = gd.astype(wire)
        gd = sent.astype(f32) + swap(sent, "dp", b ^ CROSS).astype(f32)
    return blocks, gd, grad_up


def solution(mesh):
    in_specs = (
        P(("job", "dp"), None),
        P(("job", "dp"), "panel"),
        P("job", None),
        P("job", "panel"),
        P(("job", "panel"), None),
        P(("job", "panel"), None),
        P(("job", "panel")),
    )
    out_specs = (P(("job", "panel"), "dp", None, None), P("job", "panel"), P("job", "panel"))
    return jax.shard_map(body, mesh=mesh, in_specs=in_specs, out_specs=out_specs, check_vma=False)
```

```python
import functools
import itertools

import jax
import jax.numpy as jnp
from jax import lax
from jax.experimental import pallas as pl
from jax.experimental.pallas import tpu as pltpu
from jax.sharding import PartitionSpec as P

BLK = 128
COT_CHUNK = 1024
AHEAD = 5
RADIX = 4
CROSS = 1
DOWN_WEIGHT = 40
ACT_CHUNK = 1024
LAST_LAST = (((1,), (1,)), ((), ()))
LAST_FIRST = (((1,), (0,)), ((), ()))
FIRST_FIRST = (((0,), (0,)), ((), ()))
IN_HBM = pl.BlockSpec(memory_space=pltpu.HBM)
IN_VMEM = pl.BlockSpec(memory_space=pltpu.VMEM)


def dot(a, b, dims):
    return lax.dot_general(a, b, dims, preferred_element_type=jnp.float32)


def call(kernel, outs, specs, args, scratch=(), vmem=4, flops=0, moved=0):
    return pl.pallas_call(
        kernel,
        out_shape=outs,
        in_specs=specs,
        out_specs=jax.tree.map(lambda _: IN_VMEM, outs),
        scratch_shapes=scratch,
        cost_estimate=pl.CostEstimate(flops=flops, bytes_accessed=moved, transcendentals=0),
        compiler_params=pltpu.CompilerParams(vmem_limit_bytes=vmem * 2**20),
    )(*args)


def local_kernel(rows_hbm, cols_hbm, acts, cot, down, up, sum_mine, sum_other, back,
                  rows, cols, acts_here, cot_here, down_here, up_here, act_sems, cot_sems, sems):
    dp, core = lax.axis_size("dp"), lax.rem(lax.axis_index("dp"), 2)
    width, features = acts.shape[1], cot.shape[1]
    act_step, cot_step = min(ACT_CHUNK, width), min(COT_CHUNK, features)

    def stream(source, target, step, sem):
        chunks = [pl.ds(j * step, step) for j in range(source.shape[1] // step)]
        return [pltpu.make_async_copy(source.at[:, at], target.at[:, at], sem.at[j]) for j, at in enumerate(chunks)]

    factors = [
        pltpu.make_async_copy(down, down_here, sems.at[0]),
        pltpu.make_async_copy(up, up_here, sems.at[1]),
        pltpu.make_async_copy(rows_hbm, rows, sems.at[2]),
        pltpu.make_async_copy(cols_hbm, cols, sems.at[3]),
    ]
    act_copies = stream(acts, acts_here, act_step, act_sems)
    cot_copies = stream(cot, cot_here, cot_step, cot_sems)
    order = factors + act_copies + cot_copies
    for copy in order[: AHEAD + len(factors)]:
        copy.start()
    waiting = iter(order[AHEAD + len(factors) :])

    def arrive(copy):
        copy.wait()
        for later in itertools.islice(waiting, 1):
            later.start()

    for copy in factors:
        copy.wait()
    low = None
    for j, copy in enumerate(act_copies):
        arrive(copy)
        at = pl.ds(j * act_step, act_step)
        part = dot(down_here[:, at], acts_here[:, at], LAST_LAST)
        low = part if low is None else low + part
    low = low.astype(jnp.bfloat16)
    total = None
    for j, copy in enumerate(cot_copies):
        arrive(copy)
        at = pl.ds(j * cot_step, cot_step)
        part = dot(up_here[:, at], cot_here[:, at], LAST_LAST)
        total = part if total is None else total + part
        part = dot(low, cot_here[:, at], LAST_FIRST)
        first, second = part[: part.shape[0] // 2], part[part.shape[0] // 2 :]
        sum_mine[:, at] = jnp.where(core == 0, first, second)
        sum_other[:, at] = jnp.where(core == 0, second, first)
    back[...] = total
    chips, own = dp // 2, rows.shape[1] // dp
    for out, owner in ((sum_other, 1 - core), (sum_mine, core)):
        for chip in range(chips):
            for k in range(own):
                s = (2 * chip + owner) * own + k
                r = pl.ds(pl.multiple_of(rows[0, s] * BLK, BLK), BLK)
                c = pl.ds(pl.multiple_of(cols[0, s] * BLK, BLK), BLK)
                product = dot(acts_here[:, r], cot_here[:, c], FIRST_FIRST)
                for t in range(BLK // 8):
                    at = features + ((chip * own + k) * (BLK // 8) + t) * BLK
                    out[:, at : at + BLK] = product[8 * t : 8 * t + 8]


def fetch_kernel(acts, _, out, sems):
    width, parts = out.shape[1], sems.shape[0]
    at = pl.ds(pl.multiple_of(lax.axis_index("panel") * width, width), width)
    rows = out.shape[0] // parts
    copies = []
    for j in range(parts):
        part = pl.ds(j * rows, rows)
        copies.append(pltpu.make_async_copy(acts.at[part, at], out.at[part, :], sems.at[j]))
        copies[-1].start()
    for copy in copies:
        copy.wait()


def down_kernel(*refs):
    *shares, acts, out = refs
    back = shares[0][...]
    for share in shares[1:]:
        back = back + share[...]
    out[...] = dot(back.astype(jnp.bfloat16), acts[...], LAST_FIRST)


def add_kernel(a, b, out):
    out[...] = a[...] + b[...]


def swap(x, axis, bits):
    return lax.ppermute(x, axis, [(i, i ^ bits) for i in range(lax.axis_size(axis))])


def body(acts, cot, down, up, rows, cols, live):
    tokens, width = acts.shape
    features = cot.shape[1]
    slots = rows.shape[1]
    rank = down.shape[0]
    dp, panels = lax.axis_size("dp"), lax.axis_size("panel")
    me = lax.axis_index("dp")
    core, own, mine = me % 2, slots // dp, width // panels
    f32, bf16 = jnp.float32, jnp.bfloat16
    far = [1 << b for b in range(1, dp.bit_length() - 1)]
    wire = bf16 if len(far) == 1 else f32

    hbm = functools.partial(pltpu.with_memory_space_constraint, memory_space=pltpu.HBM)
    vmem = functools.partial(pltpu.with_memory_space_constraint, memory_space=pltpu.VMEM)
    half, blk = rank // 2, BLK * BLK // 8
    here, there, back = call(
        local_kernel,
        (
            pltpu.VMEM((half, features + slots // 2 * blk), f32),
            pltpu.VMEM((half, features + slots // 2 * blk), f32),
            pltpu.VMEM((rank, tokens), f32),
        ),
        [IN_HBM] * 6,
        (hbm(rows), hbm(cols), hbm(acts), hbm(cot), hbm(down), hbm(up)),
        [
            pltpu.SMEM((1, slots), jnp.int32),
            pltpu.SMEM((1, slots), jnp.int32),
            pltpu.VMEM((tokens, width), bf16),
            pltpu.VMEM((tokens, features), bf16),
            pltpu.VMEM((rank, width), bf16),
            pltpu.VMEM((rank, features), bf16),
            pltpu.SemaphoreType.DMA((width // min(ACT_CHUNK, width),)),
            pltpu.SemaphoreType.DMA((features // min(COT_CHUNK, features),)),
            pltpu.SemaphoreType.DMA((4,)),
        ],
        vmem=24,
        flops=2 * 256 * tokens * (2 * features + width),
        moved=2 * tokens * (features + width),
    )

    bit, shares = 1, [back]
    while bit < panels:
        base = functools.reduce(jnp.add, shares)
        radix = min(RADIX, panels // bit)
        shares = [base] + [swap(base, "panel", k * bit) for k in reversed(range(1, radix))]
        bit *= radix
    got = swap(there, "dp", 1)
    total = call(
        add_kernel, pltpu.VMEM(here.shape, f32), [IN_VMEM] * 2, (vmem(here), vmem(got)), moved=3 * 4 * here.size
    )
    gu, blocks = total[:, :features], total[:, features:]
    first = None
    for b in reversed(far):
        width_left = blocks.shape[1] // 2
        side = (me // b) % 2
        away = lax.dynamic_slice_in_dim(blocks, (1 - side) * width_left, width_left, 1)
        stay = lax.dynamic_slice_in_dim(blocks, side * width_left, width_left, 1)
        sent = jnp.concatenate([gu.astype(wire), away.astype(wire)], 1)
        first = sent if first is None else first
        got = swap(sent, "dp", b)
        last, got = got, got.astype(f32)
        gu, blocks = sent[:, :features].astype(f32) + got[:, :features], stay + got[:, features:]
    blocks = blocks.reshape(8, own, BLK // 8, BLK).transpose(1, 2, 0, 3).reshape(own, BLK, BLK)
    alive = me * own + jnp.arange(own, dtype=jnp.int32) < live[0]
    blocks = jnp.where(alive[:, None, None], blocks, f32(0.0))
    other = swap(gu, "dp", 1)
    grad_up = jnp.where(core == 0, jnp.concatenate([gu, other]), jnp.concatenate([other, gu]))

    acts_mine = call(
        fetch_kernel,
        pltpu.VMEM((tokens, mine), bf16),
        [IN_HBM, pl.BlockSpec(memory_space=pl.ANY)],
        (hbm(acts), first),
        [pltpu.SemaphoreType.DMA((4,))],
        moved=2 * 2 * tokens * mine,
    )
    gd = call(
        down_kernel,
        pltpu.VMEM((rank, mine), f32),
        [IN_VMEM] * (len(shares) + 1),
        (*shares, vmem(acts_mine)),
        flops=DOWN_WEIGHT * 2 * 256 * tokens * mine,
        moved=2 * tokens * mine,
    )
    gd = gd + swap(gd, "dp", 1)
    gd, last = lax.optimization_barrier((gd, last))
    for b in far:
        sent = gd.astype(wire)
        got = swap(sent, "dp", b ^ CROSS)
        if b == far[-1]:
            got, blocks, grad_up = lax.optimization_barrier((got, blocks, grad_up))
        gd = sent.astype(f32) + got.astype(f32)
    return blocks[None], gd, grad_up


def solution(mesh):
    in_specs = (
        P(("job", "dp"), None),
        P(("job", "dp"), "panel"),
        P("job", None),
        P("job", "panel"),
        P(("job", "panel"), None),
        P(("job", "panel"), None),
        P(("job", "panel")),
    )
    out_specs = (P(("job", "panel"), "dp", None, None), P("job", "panel"), P("job", "panel"))
    return jax.shard_map(body, mesh=mesh, in_specs=in_specs, out_specs=out_specs, check_vma=False)
```

```python
import functools
import itertools

import jax
import jax.numpy as jnp
from jax import lax
from jax.experimental import pallas as pl
from jax.experimental.pallas import tpu as pltpu
from jax.sharding import PartitionSpec as P

BLK = 128
COT_CHUNK = 1024
AHEAD = 4
GROW = 2
RADIX = 2
CROSS = 1
DOWN_WEIGHT = 0
ACT_CHUNK = 1024
LAST_LAST = (((1,), (1,)), ((), ()))
LAST_FIRST = (((1,), (0,)), ((), ()))
FIRST_FIRST = (((0,), (0,)), ((), ()))
IN_HBM = pl.BlockSpec(memory_space=pltpu.HBM)
IN_VMEM = pl.BlockSpec(memory_space=pltpu.VMEM)


def dot(a, b, dims):
    return lax.dot_general(a, b, dims, preferred_element_type=jnp.float32)


def call(kernel, outs, specs, args, scratch=(), vmem=4, flops=0, moved=0):
    return pl.pallas_call(
        kernel,
        out_shape=outs,
        in_specs=specs,
        out_specs=jax.tree.map(lambda _: IN_VMEM, outs),
        scratch_shapes=scratch,
        cost_estimate=pl.CostEstimate(flops=flops, bytes_accessed=moved, transcendentals=0),
        compiler_params=pltpu.CompilerParams(vmem_limit_bytes=vmem * 2**20),
    )(*args)


def local_kernel(rows_hbm, cols_hbm, acts, cot, down, up, sum_mine, sum_other, back,
                  rows, cols, acts_here, cot_here, down_here, up_here, act_sems, cot_sems, sems):
    dp, core = lax.axis_size("dp"), lax.rem(lax.axis_index("dp"), 2)
    width, features = acts.shape[1], cot.shape[1]
    act_step, cot_step = min(ACT_CHUNK, width), min(COT_CHUNK, features)

    def stream(source, target, step, sem):
        chunks = [pl.ds(j * step, step) for j in range(source.shape[1] // step)]
        return [pltpu.make_async_copy(source.at[:, at], target.at[:, at], sem.at[j]) for j, at in enumerate(chunks)]

    factors = [
        pltpu.make_async_copy(down, down_here, sems.at[0]),
        pltpu.make_async_copy(up, up_here, sems.at[1]),
        pltpu.make_async_copy(rows_hbm, rows, sems.at[2]),
        pltpu.make_async_copy(cols_hbm, cols, sems.at[3]),
    ]
    act_copies = stream(acts, acts_here, act_step, act_sems)
    cot_copies = stream(cot, cot_here, cot_step, cot_sems)
    order = factors + act_copies + cot_copies
    for copy in order[: AHEAD + len(factors)]:
        copy.start()
    waiting = iter(order[AHEAD + len(factors) :])

    def arrive(copy):
        copy.wait()
        for later in itertools.islice(waiting, GROW):
            later.start()

    for copy in factors:
        copy.wait()
    low = None
    for j, copy in enumerate(act_copies):
        arrive(copy)
        at = pl.ds(j * act_step, act_step)
        part = dot(down_here[:, at], acts_here[:, at], LAST_LAST)
        low = part if low is None else low + part
    rank = low.shape[0]
    low = jnp.where(core == 0, low, jnp.concatenate([low[rank // 2 :], low[: rank // 2]])).astype(jnp.bfloat16)
    total = None
    for j, copy in enumerate(cot_copies):
        arrive(copy)
        at = pl.ds(j * cot_step, cot_step)
        part = dot(up_here[:, at], cot_here[:, at], LAST_LAST)
        total = part if total is None else total + part
        part = dot(low, cot_here[:, at], LAST_FIRST)
        sum_mine[:, at] = part[: rank // 2]
        sum_other[:, at] = part[rank // 2 :]
    back[...] = total
    chips, own = dp // 2, rows.shape[1] // dp
    for out, owner in ((sum_other, 1 - core), (sum_mine, core)):
        for chip in range(chips):
            for k in range(own):
                s = (2 * chip + owner) * own + k
                r = pl.ds(pl.multiple_of(rows[0, s] * BLK, BLK), BLK)
                c = pl.ds(pl.multiple_of(cols[0, s] * BLK, BLK), BLK)
                product = dot(acts_here[:, r], cot_here[:, c], FIRST_FIRST)
                for t in range(BLK // 8):
                    at = features + ((chip * own + k) * (BLK // 8) + t) * BLK
                    out[:, at : at + BLK] = product[8 * t : 8 * t + 8]


def fetch_kernel(acts, _, out, sems):
    width, parts = out.shape[1], sems.shape[0]
    at = pl.ds(pl.multiple_of(lax.axis_index("panel") * width, width), width)
    rows = out.shape[0] // parts
    copies = []
    for j in range(parts):
        part = pl.ds(j * rows, rows)
        copies.append(pltpu.make_async_copy(acts.at[part, at], out.at[part, :], sems.at[j]))
        copies[-1].start()
    for copy in copies:
        copy.wait()


def down_kernel(*refs):
    *shares, acts, out = refs
    back = shares[0][...]
    for share in shares[1:]:
        back = back + share[...]
    out[...] = dot(back.astype(jnp.bfloat16), acts[...], LAST_FIRST)


def add_kernel(a, b, out):
    out[...] = a[...] + b[...]


def swap(x, axis, bits):
    return lax.ppermute(x, axis, [(i, i ^ bits) for i in range(lax.axis_size(axis))])


def body(acts, cot, down, up, rows, cols, live):
    tokens, width = acts.shape
    features = cot.shape[1]
    slots = rows.shape[1]
    rank = down.shape[0]
    dp, panels = lax.axis_size("dp"), lax.axis_size("panel")
    me = lax.axis_index("dp")
    core, own, mine = me % 2, slots // dp, width // panels
    f32, bf16 = jnp.float32, jnp.bfloat16
    far = [1 << b for b in range(1, dp.bit_length() - 1)]
    wire = bf16 if len(far) == 1 else f32

    hbm = functools.partial(pltpu.with_memory_space_constraint, memory_space=pltpu.HBM)
    vmem = functools.partial(pltpu.with_memory_space_constraint, memory_space=pltpu.VMEM)
    half, blk = rank // 2, BLK * BLK // 8
    here, there, back = call(
        local_kernel,
        (
            pltpu.VMEM((half, features + slots // 2 * blk), f32),
            pltpu.VMEM((half, features + slots // 2 * blk), f32),
            pltpu.VMEM((rank, tokens), f32),
        ),
        [IN_HBM] * 6,
        (hbm(rows), hbm(cols), hbm(acts), hbm(cot), hbm(down), hbm(up)),
        [
            pltpu.SMEM((1, slots), jnp.int32),
            pltpu.SMEM((1, slots), jnp.int32),
            pltpu.VMEM((tokens, width), bf16),
            pltpu.VMEM((tokens, features), bf16),
            pltpu.VMEM((rank, width), bf16),
            pltpu.VMEM((rank, features), bf16),
            pltpu.SemaphoreType.DMA((width // min(ACT_CHUNK, width),)),
            pltpu.SemaphoreType.DMA((features // min(COT_CHUNK, features),)),
            pltpu.SemaphoreType.DMA((4,)),
        ],
        vmem=24,
        flops=2 * 256 * tokens * (2 * features + width),
        moved=2 * tokens * (features + width),
    )

    got = swap(there, "dp", 1)
    total = call(
        add_kernel, pltpu.VMEM(here.shape, f32), [IN_VMEM] * 2, (vmem(here), vmem(got)), moved=3 * 4 * here.size
    )
    gu, blocks = total[:, :features], total[:, features:]
    first = None
    for b in reversed(far):
        width_left = blocks.shape[1] // 2
        side = (me // b) % 2
        away = lax.dynamic_slice_in_dim(blocks, (1 - side) * width_left, width_left, 1)
        stay = lax.dynamic_slice_in_dim(blocks, side * width_left, width_left, 1)
        sent = jnp.concatenate([gu.astype(wire), away.astype(wire)], 1)
        first = sent if first is None else first
        got = swap(sent, "dp", b)
        last, got = got, got.astype(f32)
        gu, blocks = sent[:, :features].astype(f32) + got[:, :features], stay + got[:, features:]
    blocks = blocks.reshape(8, own, BLK // 8, BLK).transpose(1, 2, 0, 3).reshape(own, BLK, BLK)
    alive = me * own + jnp.arange(own, dtype=jnp.int32) < live[0]
    blocks = jnp.where(alive[:, None, None], blocks, f32(0.0))
    other = swap(gu, "dp", 1)
    grad_up = jnp.where(core == 0, jnp.concatenate([gu, other]), jnp.concatenate([other, gu]))

    bit, shares = 1, [back]
    while bit < panels:
        if bit > 1:
            shares[-1], first = lax.optimization_barrier((shares[-1], first))
        base = functools.reduce(jnp.add, shares)
        radix = min(RADIX, panels // bit)
        shares = [base] + [swap(base, "panel", (panels // 2) // bit) for k in reversed(range(1, radix))]
        bit *= radix
    acts_mine = call(
        fetch_kernel,
        pltpu.VMEM((tokens, mine), bf16),
        [IN_HBM, pl.BlockSpec(memory_space=pl.ANY)],
        (hbm(acts), shares[0]),
        [pltpu.SemaphoreType.DMA((4,))],
        moved=2 * 2 * tokens * mine,
    )
    gd = call(
        down_kernel,
        pltpu.VMEM((rank, mine), f32),
        [IN_VMEM] * (len(shares) + 1),
        (*shares, vmem(acts_mine)),
        flops=DOWN_WEIGHT * 2 * 256 * tokens * mine,
        moved=2 * tokens * mine,
    )
    gd = gd + swap(gd, "dp", 1)
    gd, last = lax.optimization_barrier((gd, last))
    for b in far:
        sent = gd.astype(wire)
        got = swap(sent, "dp", b ^ CROSS)
        if b == far[-1]:
            got, blocks, grad_up = lax.optimization_barrier((got, blocks, grad_up))
        gd = sent.astype(f32) + got.astype(f32)
    return blocks[None], gd, grad_up


def solution(mesh):
    in_specs = (
        P(("job", "dp"), None),
        P(("job", "dp"), "panel"),
        P("job", None),
        P("job", "panel"),
        P(("job", "panel"), None),
        P(("job", "panel"), None),
        P(("job", "panel")),
    )
    out_specs = (P(("job", "panel"), "dp", None, None), P("job", "panel"), P("job", "panel"))
    return jax.shard_map(body, mesh=mesh, in_specs=in_specs, out_specs=out_specs, check_vma=False)
```

```python
import functools
import itertools

import jax
import jax.numpy as jnp
from jax import lax
from jax.experimental import pallas as pl
from jax.experimental.pallas import tpu as pltpu
from jax.sharding import PartitionSpec as P

BLK = 128
COT_CHUNK = 1024
AHEAD = 4
GROW = 2
RADIX = 2
CROSS = 1
DOWN_WEIGHT = 0
ACT_CHUNK = 1024
LAST_LAST = (((1,), (1,)), ((), ()))
LAST_FIRST = (((1,), (0,)), ((), ()))
FIRST_FIRST = (((0,), (0,)), ((), ()))
IN_HBM = pl.BlockSpec(memory_space=pltpu.HBM)
IN_VMEM = pl.BlockSpec(memory_space=pltpu.VMEM)


def dot(a, b, dims):
    return lax.dot_general(a, b, dims, preferred_element_type=jnp.float32)


def call(kernel, outs, specs, args, scratch=(), vmem=4, flops=0, moved=0):
    return pl.pallas_call(
        kernel,
        out_shape=outs,
        in_specs=specs,
        out_specs=jax.tree.map(lambda _: IN_VMEM, outs),
        scratch_shapes=scratch,
        cost_estimate=pl.CostEstimate(flops=flops, bytes_accessed=moved, transcendentals=0),
        compiler_params=pltpu.CompilerParams(vmem_limit_bytes=vmem * 2**20),
    )(*args)


def local_kernel(rows_hbm, cols_hbm, acts, cot, down, up, sum_mine, sum_other, back,
                  rows, cols, acts_here, cot_here, down_here, up_here, act_sems, cot_sems, sems):
    dp, core = lax.axis_size("dp"), lax.rem(lax.axis_index("dp"), 2)
    width, features = acts.shape[1], cot.shape[1]
    act_step, cot_step = min(ACT_CHUNK, width), min(COT_CHUNK, features)

    def stream(source, target, step, sem):
        chunks = [pl.ds(j * step, step) for j in range(source.shape[1] // step)]
        return [pltpu.make_async_copy(source.at[:, at], target.at[:, at], sem.at[j]) for j, at in enumerate(chunks)]

    factors = [
        pltpu.make_async_copy(down, down_here, sems.at[0]),
        pltpu.make_async_copy(up, up_here, sems.at[1]),
        pltpu.make_async_copy(rows_hbm, rows, sems.at[2]),
        pltpu.make_async_copy(cols_hbm, cols, sems.at[3]),
    ]
    act_copies = stream(acts, acts_here, act_step, act_sems)
    cot_copies = stream(cot, cot_here, cot_step, cot_sems)
    order = factors + act_copies + cot_copies
    for copy in order[: AHEAD + len(factors)]:
        copy.start()
    waiting = iter(order[AHEAD + len(factors) :])

    def arrive(copy):
        copy.wait()
        for later in itertools.islice(waiting, GROW):
            later.start()

    for copy in factors:
        copy.wait()
    low = None
    for j, copy in enumerate(act_copies):
        arrive(copy)
        at = pl.ds(j * act_step, act_step)
        part = dot(down_here[:, at], acts_here[:, at], LAST_LAST)
        low = part if low is None else low + part
    rank = low.shape[0]
    low = jnp.where(core == 0, low, jnp.concatenate([low[rank // 2 :], low[: rank // 2]])).astype(jnp.bfloat16)
    total = None
    for j, copy in enumerate(cot_copies):
        arrive(copy)
        at = pl.ds(j * cot_step, cot_step)
        part = dot(up_here[:, at], cot_here[:, at], LAST_LAST)
        total = part if total is None else total + part
        part = dot(low, cot_here[:, at], LAST_FIRST)
        sum_mine[:, at] = part[: rank // 2]
        sum_other[:, at] = part[rank // 2 :]
    back[...] = total
    chips, own = dp // 2, rows.shape[1] // dp
    for out, owner in ((sum_other, 1 - core), (sum_mine, core)):
        for chip in range(chips):
            for k in range(own):
                s = (2 * chip + owner) * own + k
                r = pl.ds(pl.multiple_of(rows[0, s] * BLK, BLK), BLK)
                c = pl.ds(pl.multiple_of(cols[0, s] * BLK, BLK), BLK)
                product = dot(acts_here[:, r], cot_here[:, c], FIRST_FIRST)
                for t in range(BLK // 8):
                    at = features + ((chip * own + k) * (BLK // 8) + t) * BLK
                    out[:, at : at + BLK] = product[8 * t : 8 * t + 8]


def fetch_kernel(acts, _, out, sems):
    width, parts = out.shape[1], sems.shape[0]
    at = pl.ds(pl.multiple_of(lax.axis_index("panel") * width, width), width)
    rows = out.shape[0] // parts
    copies = []
    for j in range(parts):
        part = pl.ds(j * rows, rows)
        copies.append(pltpu.make_async_copy(acts.at[part, at], out.at[part, :], sems.at[j]))
        copies[-1].start()
    for copy in copies:
        copy.wait()


def down_kernel(*refs):
    *shares, acts, out = refs
    back = shares[0][...]
    for share in shares[1:]:
        back = back + share[...]
    out[...] = dot(back.astype(jnp.bfloat16), acts[...], LAST_FIRST)


def add_kernel(a, b, out):
    out[...] = a[...] + b[...]


def swap(x, axis, bits):
    return lax.ppermute(x, axis, [(i, i ^ bits) for i in range(lax.axis_size(axis))])


def body(acts, cot, down, up, rows, cols, live):
    tokens, width = acts.shape
    features = cot.shape[1]
    slots = rows.shape[1]
    rank = down.shape[0]
    dp, panels = lax.axis_size("dp"), lax.axis_size("panel")
    me = lax.axis_index("dp")
    core, own, mine = me % 2, slots // dp, width // panels
    f32, bf16 = jnp.float32, jnp.bfloat16
    far = [1 << b for b in range(1, dp.bit_length() - 1)]
    wire = bf16 if len(far) == 1 else f32

    hbm = functools.partial(pltpu.with_memory_space_constraint, memory_space=pltpu.HBM)
    vmem = functools.partial(pltpu.with_memory_space_constraint, memory_space=pltpu.VMEM)
    half, blk = rank // 2, BLK * BLK // 8
    here, there, back = call(
        local_kernel,
        (
            pltpu.VMEM((half, features + slots // 2 * blk), f32),
            pltpu.VMEM((half, features + slots // 2 * blk), f32),
            pltpu.VMEM((rank, tokens), f32),
        ),
        [IN_HBM] * 6,
        (hbm(rows), hbm(cols), hbm(acts), hbm(cot), hbm(down), hbm(up)),
        [
            pltpu.SMEM((1, slots), jnp.int32),
            pltpu.SMEM((1, slots), jnp.int32),
            pltpu.VMEM((tokens, width), bf16),
            pltpu.VMEM((tokens, features), bf16),
            pltpu.VMEM((rank, width), bf16),
            pltpu.VMEM((rank, features), bf16),
            pltpu.SemaphoreType.DMA((width // min(ACT_CHUNK, width),)),
            pltpu.SemaphoreType.DMA((features // min(COT_CHUNK, features),)),
            pltpu.SemaphoreType.DMA((4,)),
        ],
        vmem=24,
        flops=2 * 256 * tokens * (2 * features + width),
        moved=2 * tokens * (features + width),
    )

    got = swap(there, "dp", 1)
    total = call(
        add_kernel, pltpu.VMEM(here.shape, f32), [IN_VMEM] * 2, (vmem(here), vmem(got)), moved=3 * 4 * here.size
    )
    gu, blocks = total[:, :features], total[:, features:]
    first = None
    for b in reversed(far):
        width_left = blocks.shape[1] // 2
        side = (me // b) % 2
        away = lax.dynamic_slice_in_dim(blocks, (1 - side) * width_left, width_left, 1)
        stay = lax.dynamic_slice_in_dim(blocks, side * width_left, width_left, 1)
        sent = jnp.concatenate([gu.astype(wire), away.astype(wire)], 1)
        first = sent if first is None else first
        got = swap(sent, "dp", b)
        last, got = got, got.astype(f32)
        gu, blocks = sent[:, :features].astype(f32) + got[:, :features], stay + got[:, features:]
    blocks = blocks.reshape(8, own, BLK // 8, BLK).transpose(1, 2, 0, 3).reshape(own, BLK, BLK)
    alive = me * own + jnp.arange(own, dtype=jnp.int32) < live[0]
    blocks = jnp.where(alive[:, None, None], blocks, f32(0.0))

    bit, shares = 1, [back]
    while bit < panels:
        if bit > 1:
            shares[-1], first = lax.optimization_barrier((shares[-1], first))
        base = functools.reduce(jnp.add, shares)
        radix = min(RADIX, panels // bit)
        shares = [base] + [swap(base, "panel", (panels // 2) // bit) for k in reversed(range(1, radix))]
        bit *= radix
    acts_mine = call(
        fetch_kernel,
        pltpu.VMEM((tokens, mine), bf16),
        [IN_HBM, pl.BlockSpec(memory_space=pl.ANY)],
        (hbm(acts), shares[0]),
        [pltpu.SemaphoreType.DMA((4,))],
        moved=2 * 2 * tokens * mine,
    )
    gd = call(
        down_kernel,
        pltpu.VMEM((rank, mine), f32),
        [IN_VMEM] * (len(shares) + 1),
        (*shares, vmem(acts_mine)),
        flops=DOWN_WEIGHT * 2 * 256 * tokens * mine,
        moved=2 * tokens * mine,
    )
    gd = gd + swap(gd, "dp", 1)
    gd, last = lax.optimization_barrier((gd, last))
    gu, _ = lax.optimization_barrier((gu, gd.astype(wire)))
    other = swap(gu, "dp", 1)
    grad_up = jnp.where(core == 0, jnp.concatenate([gu, other]), jnp.concatenate([other, gu]))
    for b in far:
        sent = gd.astype(wire)
        got = swap(sent, "dp", b ^ CROSS)
        if b == far[-1]:
            got, blocks, grad_up = lax.optimization_barrier((got, blocks, grad_up))
        gd = sent.astype(f32) + got.astype(f32)
    return blocks[None], gd, grad_up


def solution(mesh):
    in_specs = (
        P(("job", "dp"), None),
        P(("job", "dp"), "panel"),
        P("job", None),
        P("job", "panel"),
        P(("job", "panel"), None),
        P(("job", "panel"), None),
        P(("job", "panel")),
    )
    out_specs = (P(("job", "panel"), "dp", None, None), P("job", "panel"), P("job", "panel"))
    return jax.shard_map(body, mesh=mesh, in_specs=in_specs, out_specs=out_specs, check_vma=False)
```
